32 devices in a mesh: seq: 8 (over y, x, core), fsdp: 4 (over z).
Axes of the slice: x: 2, y: 2, z: 4, core: 2. Of those that a mesh axis runs over, the one named last changes fastest.
Arguments:
- tokens: bfloat16 [4096, 4096], P('seq'), may hold values from -6 to 6
- w_in: bfloat16 [4096, 3072], P('seq', 'fsdp'), may hold values from -0.09375 to 0.09375
- step_logit: float32 [4096, 16], P('seq', 'fsdp'), may hold values from -7 to -5.5
- decay_logit: float32 [4096, 16], P('seq', 'fsdp'), may hold values from -20 to 1
- cotangent: bfloat16 [4096, 2048], P('seq', 'fsdp'), may hold values from -0.375 to 0.375
Outputs:
- layer_out: float32 [4096, 2048], P('seq', 'fsdp')
- input_grad: bfloat16 [4096, 4096], P('fsdp', 'seq')
- w_in_grad: float32 [4096, 3072], P('seq', 'fsdp')
The draws below stay inside these ranges and needn't reach their ends.
All inputs are finite; a program needn't handle non-finite values.
Results may differ from the reference program's by a relative error of at most 0.017.
Values may be sent and summed in bfloat16 or wider, within the bound.
No kernel may reach another device: no remote copies, remote signals or barrier semaphores. Data moves between devices by JAX's collectives and lax.ppermute only.
A program may use at most 128 MiB of HBM per device.

```python
import jax
import jax.numpy as jnp
from jax import lax

D = 4096
HEAD_DIM = 128
STATE = 128
HEADS_DEV = 4
BLOCK = 128
TOK_DEV = 512
TOKEN_TOTAL = 4096
GROUPS = 4
HEAD_TOTAL = 16
INNER = 2048
COLS_DEV = 768


def draw_decay_logit(key, part):
    random_keys = jax.random.split(jax.random.fold_in(key, 17), 6)
    fast_cut = 5
    quick_heads = jax.random.randint(random_keys[0], (1, HEAD_TOTAL), 0, 10) < fast_cut
    shard_count = TOKEN_TOTAL // TOK_DEV
    shard_factor = jnp.exp(jax.random.uniform(random_keys[1], (shard_count, 1, HEAD_TOTAL), jnp.float32, -0.7, 0.7))
    shard_factor = jnp.broadcast_to(shard_factor, (shard_count, TOK_DEV, HEAD_TOTAL)).reshape(TOKEN_TOTAL, HEAD_TOTAL)
    rough = jnp.exp(jax.random.uniform(random_keys[2], (TOKEN_TOTAL, HEAD_TOTAL), jnp.float32, -0.4, 0.4))
    gentle_frequency = 0.06 / TOKEN_TOTAL * shard_factor * rough
    quick_frequency = jax.random.uniform(random_keys[3], (1, HEAD_TOTAL), jnp.float32, 0.02, 0.033) * shard_factor * rough
    spike_locations = jax.random.randint(random_keys[4], (3, HEAD_TOTAL), 0, TOKEN_TOTAL)
    token_positions = jnp.arange(TOKEN_TOTAL, dtype=jnp.int32)
    spike_hits = jnp.any(token_positions[:, None, None] == spike_locations[None], axis=1)
    spike_frequency = jax.random.uniform(random_keys[5], (TOKEN_TOTAL, HEAD_TOTAL), jnp.float32, 0.22, 0.69)
    base_frequency = jnp.where(quick_heads, quick_frequency, jnp.where(spike_hits, spike_frequency, gentle_frequency))
    return jnp.log(jnp.expm1(base_frequency)).astype(jnp.float32)


def block_levels(rng, dims, cuts, low, top_value):
    factor_of = 1.0
    for dim, shards_of in cuts:
        steps = jax.random.uniform(jax.random.fold_in(jax.random.fold_in(rng, 6), dim), (shards_of,), jnp.float32, low / len(cuts), top_value / len(cuts))
        factor_of = factor_of * jnp.repeat(jnp.exp(steps), dims[dim] // shards_of).reshape((-1,) + (1,) * (len(dims) - 1 - dim))
    return factor_of


def scatter_about(stream_key, dims, deviation, limit, shards=(), kind=jnp.bfloat16):
    values = deviation * jax.random.normal(stream_key, dims, jnp.float32)
    if shards:
        values = values * block_levels(stream_key, dims, shards, -0.22, 0.18)
    return jnp.clip(values, -limit, limit).astype(kind)


def setup_inputs(seed: int = 0) -> dict:
    splits = jax.random.split(jax.random.key(seed), 6)
    return {
        "tokens": scatter_about(splits[0], (TOKEN_TOTAL, D), 1.0, 6.0, ((0, 8),)),
        "w_in": scatter_about(splits[1], (D, GROUPS * COLS_DEV), D ** -0.5, 0.09375, ((0, 8), (1, 4))),
        "step_logit": jnp.clip(-7.0 + 1.5 * jax.random.uniform(splits[2], (TOKEN_TOTAL, HEAD_TOTAL), jnp.float32) ** block_levels(splits[2], (TOKEN_TOTAL, HEAD_TOTAL), ((0, 8), (1, 4)), -0.2, 0.2), -7.0, -5.5),
        "decay_logit": draw_decay_logit(jax.random.fold_in(splits[5], 71), 0),
        "cotangent": scatter_about(splits[4], (TOKEN_TOTAL, INNER), 0.0625, 0.375, ((0, 8), (1, 4))),
    }


def block_step(memory, inputs):
    values, in_map, out_map, step_size, log_decay = inputs
    cum_decay = jnp.cumsum(log_decay, axis=0)
    scores = jnp.einsum('tgn,sgn->gts', out_map, in_map, preferred_element_type=jnp.float32)
    along = jnp.moveaxis(cum_decay, 0, -1)
    steps_along = jnp.moveaxis(step_size, 0, -1)
    span = along.shape[-1]
    causal = lax.broadcasted_iota(jnp.int32, (span, span), 0) >= lax.broadcasted_iota(jnp.int32, (span, span), 1)
    decays = jnp.exp(jnp.where(causal, along[..., :, None] - along[..., None, :], -1e+30))
    mixing = (scores[:, None] * decays * steps_along[..., None, :]).astype(jnp.bfloat16)
    local_out = jnp.einsum('ghts,sghp->tghp', mixing, values, preferred_element_type=jnp.float32)
    carried = jnp.einsum('tgn,ghnp->tghp', out_map.astype(jnp.float32), memory, precision=lax.Precision.HIGHEST)
    outputs = local_out + jnp.exp(cum_decay)[..., None] * carried
    block_total = cum_decay[-1]
    weight_end = jnp.exp(block_total[None] - cum_decay) * step_size
    scaled_in = (in_map.astype(jnp.float32)[:, :, None, :] * weight_end[..., None]).astype(jnp.bfloat16)
    written = jnp.einsum('sghn,sghp->ghnp', scaled_in, values, preferred_element_type=jnp.float32)
    return (jnp.exp(block_total)[..., None, None] * memory + written, outputs)

def run_blocks(projected, step_size, log_decay, groups):
    rows = projected.shape[0]
    block_count = rows // BLOCK
    width = HEADS_DEV * HEAD_DIM
    grouped = projected.reshape(rows, groups, width + 2 * STATE)
    values = grouped[:, :, :width].reshape(block_count, BLOCK, groups, HEADS_DEV, HEAD_DIM)
    in_map = grouped[:, :, width:width + STATE].reshape(block_count, BLOCK, groups, STATE)
    out_map = grouped[:, :, width + STATE:].reshape(block_count, BLOCK, groups, STATE)
    steps_blocked = step_size.reshape(block_count, BLOCK, groups, HEADS_DEV)
    decay_blocked = log_decay.reshape(block_count, BLOCK, groups, HEADS_DEV)
    empty_state = jnp.zeros((groups, HEADS_DEV, STATE, HEAD_DIM), jnp.float32)
    final_state, outputs = lax.scan(block_step, empty_state, (values, in_map, out_map, steps_blocked, decay_blocked))
    return (outputs.reshape(rows, groups * width), final_state)

def reference(tokens, w_in, step_logit, decay_logit, cotangent):
    step_size = jax.nn.softplus(step_logit)
    log_decay = -jax.nn.softplus(decay_logit)
    projected = jnp.dot(tokens, w_in, preferred_element_type=jnp.float32).astype(jnp.bfloat16)

    def mixer(proj_in):
        return run_blocks(proj_in, step_size, log_decay, GROUPS)[0]
    layer_out, pullback = jax.vjp(mixer, projected)
    proj_grad, = pullback(cotangent.astype(jnp.float32))
    input_grad = lax.dot_general(w_in, proj_grad, (((1,), (1,)), ((), ())), preferred_element_type=jnp.float32).astype(jnp.bfloat16)
    w_in_grad = lax.dot_general(tokens, proj_grad, (((0,), (0,)), ((), ())), preferred_element_type=jnp.float32)
    return (layer_out, input_grad, w_in_grad)
```

```python
import functools

import jax
import jax.numpy as jnp
from jax import lax
from jax.experimental import pallas as pl
from jax.experimental.pallas import tpu as pltpu
from jax.sharding import PartitionSpec as P

HEAD_DIM = 128
STATE = 128
HEADS = 4
WIDTH = HEADS * HEAD_DIM
STRIP = 128

F32 = jnp.float32
BF16 = jnp.bfloat16
NN = (((1,), (0,)), ((), ()))
NT = (((1,), (1,)), ((), ()))
TN = (((0,), (0,)), ((), ()))


def mm(a, b, dims=NN):
    return lax.dot_general(a, b, dims, preferred_element_type=F32)


def call(kernel, outs, args, flops):
    moved = sum(a.size * a.dtype.itemsize for a in (*args, *outs))
    return pl.pallas_call(
        kernel,
        out_shape=outs,
        in_specs=[pl.BlockSpec(memory_space=pltpu.VMEM)] * len(args),
        out_specs=[pl.BlockSpec(memory_space=pltpu.VMEM)] * len(outs),
        compiler_params=pltpu.CompilerParams(vmem_limit_bytes=40 * 2**20),
        cost_estimate=pl.CostEstimate(flops=flops, bytes_accessed=moved, transcendentals=0),
    )(*args)


def head(h):
    return slice(h * HEAD_DIM, (h + 1) * HEAD_DIM)


def ends_kernel(proj, cot, to_end, growth, ends):
    in_map = proj[:, WIDTH : WIDTH + STATE]
    out_map = proj[:, WIDTH + STATE :]
    fed = [
        (proj[:, head(h)].astype(F32) * to_end[:, h : h + 1]).astype(BF16) for h in range(HEADS)
    ]
    grown = [
        (cot[:, head(h)].astype(F32) * growth[:, h : h + 1]).astype(BF16) for h in range(HEADS)
    ]
    ends[:STATE, :] = mm(in_map, jnp.concatenate(fed, axis=1), TN).astype(BF16)
    ends[STATE:, :] = mm(out_map, jnp.concatenate(grown, axis=1), TN).astype(BF16)


def local_kernel(
    proj, cot, cum, cum_rows, step_rows, to_end, growth, y, dx, db, dc, fed, grown
):
    rows = proj.shape[0]
    for h in range(HEADS):
        fed[:, head(h)] = (proj[:, head(h)].astype(F32) * to_end[:, h : h + 1]).astype(BF16)
        grown[:, head(h)] = (cot[:, head(h)].astype(F32) * growth[:, h : h + 1]).astype(BF16)
    dx[...] = jnp.zeros_like(dx)
    db[...] = jnp.zeros_like(db)
    for at in range(0, rows, STRIP):
        upto = at + STRIP
        here = slice(at, upto)
        in_map = proj[:upto, WIDTH : WIDTH + STATE]
        out_map = proj[here, WIDTH + STATE :]
        scores = mm(out_map, in_map, NT)
        t = lax.broadcasted_iota(jnp.int32, (STRIP, upto), 0) + at
        s = lax.broadcasted_iota(jnp.int32, (STRIP, upto), 1)
        causal = t >= s
        dscores = jnp.zeros_like(scores)
        for h in range(HEADS):
            span = cum[here, h : h + 1] - cum_rows[h : h + 1, :upto]
            factor = jnp.exp(jnp.where(causal, span, -1e30)) * step_rows[h : h + 1, :upto]
            mixing = (scores * factor).astype(BF16)
            values = proj[:upto, head(h)]
            grad = cot[here, head(h)]
            y[here, head(h)] = mm(mixing, values)
            dx[:upto, head(h)] += mm(mixing, grad, TN)
            dscores = dscores + mm(grad, values, NT) * factor
        dscores = dscores.astype(BF16)
        dc[here, :] = mm(dscores, in_map)
        db[:upto, :] += mm(dscores, out_map, TN)


def join_kernel(
    count, proj, to_end, dx, db, dc, fed, grown, weights, near, *rest
):
    far, (proj_grad, entering) = rest[:count], rest[count:]
    before = near[:STATE, :].astype(F32) * weights[0:1, :]
    after = near[STATE:, :].astype(F32) * weights[1:2, :]
    for j, part in enumerate(far):
        value = part[...].astype(F32)
        before = before + value * weights[2 * j + 2 : 2 * j + 3, :]
        after = after + value * weights[2 * j + 3 : 2 * j + 4, :]
    before = before.astype(BF16)
    after = after.astype(BF16)
    entering[...] = before
    carried = mm(proj[:, WIDTH : WIDTH + STATE], after)
    for h in range(HEADS):
        proj_grad[:, head(h)] = (dx[:, head(h)] + carried[:, head(h)] * to_end[:, h : h + 1]).astype(BF16)
    proj_grad[:, WIDTH : WIDTH + STATE] = (db[...] + mm(fed[...], after, NT)).astype(BF16)
    proj_grad[:, WIDTH + STATE :] = (dc[...] + mm(grown[...], before, NT)).astype(BF16)


def output_kernel(proj, entering, growth, y, out):
    carried = mm(proj[:, WIDTH + STATE :], entering[...])
    for h in range(HEADS):
        out[:, head(h)] = y[:, head(h)] + carried[:, head(h)] * growth[:, h : h + 1]


def swap(value, size, bit):
    return lax.ppermute(value, "seq", [(i, i ^ bit) for i in range(size)])


def spread(row):
    return jnp.repeat(row, HEAD_DIM, axis=-1)


def shards(tokens, w_in, step_logit, decay_logit, cotangent):
    size = lax.axis_size("seq")
    me = lax.axis_index("seq")
    core, chip = me % 2, me // 2
    square = size == 8
    rows, columns = tokens.shape[0], w_in.shape[1]
    part = w_in.shape[0]
    half = part // 2
    state = jax.ShapeDtypeStruct

    def token_columns(bit):
        return lax.dynamic_slice_in_dim(tokens, (me ^ bit) * part, part, axis=1)

    if square:
        from_x, from_y = swap(w_in, size, 2), swap(w_in, size, 4)
        near = swap(w_in, size, 1)
        corner0 = swap(from_x[:half], size, 4)
        corner1 = swap(from_y[half:], size, 2)
        near_x, near_y = swap(from_x, size, 1), swap(from_y, size, 1)
        near0, near1 = swap(corner0, size, 1), swap(corner1, size, 1)
        pieces = [(0, 0, w_in), (1, 0, near), (2, 0, from_x), (4, 0, from_y), (3, 0, near_x), (5, 0, near_y)]
        pieces += [(6, 0, corner0), (6, half, corner1), (7, 0, near0), (7, half, near1)]
        total = 0.0
        for bit, first, piece in pieces:
            total = total + mm(token_columns(bit)[:, first : first + piece.shape[0]], piece)
        projected = total.astype(BF16)
        gathered = jnp.zeros((part * size, columns), BF16)
        for bit, first, piece in pieces:
            gathered = lax.dynamic_update_slice_in_dim(gathered, piece, (me ^ bit) * part + first, axis=0)
    else:
        gathered = lax.all_gather(w_in, "seq", axis=0, tiled=True)
        projected = mm(tokens, gathered).astype(BF16)

    step_size = jax.nn.softplus(step_logit)
    log_decay = -jax.nn.softplus(decay_logit)
    lower = (
        lax.broadcasted_iota(jnp.int32, (rows, rows), 0) >= lax.broadcasted_iota(jnp.int32, (rows, rows), 1)
    ).astype(F32)
    cum = lax.dot_general(lower, log_decay, NN, precision=lax.Precision.HIGHEST, preferred_element_type=F32)
    log_total = cum[-1]
    growth = jnp.exp(cum)
    to_end = jnp.exp(log_total[None] - cum) * step_size
    cum_rows, step_rows = cum.T, step_size.T
    totals = lax.all_gather(log_total, "seq")

    (ends,) = call(
        ends_kernel,
        [state((2 * STATE, WIDTH), BF16)],
        [projected, cotangent, to_end, growth],
        4 * rows * STATE * WIDTH,
    )
    if square:
        other = swap(ends, size, 1)
        pair = totals.reshape(size // 2, 2, HEADS)
        of_chip = pair.sum(1)
        until = jnp.stack(
            [sum([of_chip[j] for j in range(k)], jnp.zeros((HEADS,), F32)) for k in range(size // 2 + 1)]
        )
        mine = pair[chip]
        first, second = jnp.exp(mine[0]), jnp.exp(mine[1])
        one = jnp.ones_like(first)
        own_ends = jnp.concatenate(
            [
                jnp.broadcast_to(spread(jnp.where(core == 0, second, one)), (STATE, WIDTH)),
                jnp.broadcast_to(spread(jnp.where(core == 0, one, first)), (STATE, WIDTH)),
            ]
        )
        other_ends = jnp.concatenate(
            [
                jnp.broadcast_to(spread(jnp.where(core == 0, one, second)), (STATE, WIDTH)),
                jnp.broadcast_to(spread(jnp.where(core == 0, first, one)), (STATE, WIDTH)),
            ]
        )
        both = (ends.astype(F32) * own_ends + other.astype(F32) * other_ends).astype(BF16)
        forward, backward = both[:STATE], both[STATE:]
        for_x = jnp.where(chip % 2 == 0, forward, backward)
        for_y = jnp.where(chip < 2, forward, backward)
        far = [swap(for_x, size, 2), swap(for_y, size, 4), swap(for_y, size, 6)]
        weights = [
            jnp.where(core == 1, one, 0.0),
            jnp.where(core == 0, one, 0.0),
        ]
        for bit in (1, 2, 3):
            there = chip ^ bit
            reach = jnp.where(there < chip, until[chip] - until[there + 1], -1e30)
            weights.append(jnp.exp(reach) * jnp.where(core == 1, first, one))
            reach = jnp.where(there > chip, until[there] - until[chip + 1], -1e30)
            weights.append(jnp.exp(reach) * jnp.where(core == 0, second, one))
        weights = spread(jnp.stack(weights))
    else:
        everything = lax.all_gather(ends, "seq")
        places = jnp.arange(size)
        until = jnp.stack([jnp.sum(jnp.where((places < k)[:, None], totals, 0.0), axis=0) for k in range(size + 1)])
        reach = jnp.where((places < me)[:, None], until[me][None] - until[1:], -1e30)
        before = jnp.einsum("jnk,jk->nk", everything[:, :STATE].astype(F32), spread(jnp.exp(reach)))
        reach = jnp.where((places > me)[:, None], until[:-1] - until[me + 1][None], -1e30)
        after = jnp.einsum("jnk,jk->nk", everything[:, STATE:].astype(F32), spread(jnp.exp(reach)))
        other = jnp.concatenate([before, after]).astype(BF16)
        far = []
        weights = jnp.ones((2, WIDTH), F32)

    y, dx, db, dc, fed, grown = call(
        local_kernel,
        [
            state((rows, WIDTH), F32),
            state((rows, WIDTH), F32),
            state((rows, STATE), F32),
            state((rows, STATE), F32),
            state((rows, WIDTH), BF16),
            state((rows, WIDTH), BF16),
        ],
        [projected, cotangent, cum, cum_rows, step_rows, to_end, growth],
        20 * rows * rows * STATE,
    )
    proj_grad, entering = call(
        functools.partial(join_kernel, len(far)),
        [state((rows, columns), BF16), state((STATE, WIDTH), BF16)],
        [projected, to_end, dx, db, dc, fed, grown, weights, other, *far],
        6 * rows * STATE * WIDTH,
    )
    input_grad = lax.psum_scatter(
        mm(gathered, proj_grad, NT).astype(BF16), "fsdp", scatter_dimension=0, tiled=True
    )
    (layer_out,) = call(
        output_kernel,
        [state((rows, WIDTH), F32)],
        [projected, entering, growth, y],
        2 * rows * STATE * WIDTH,
    )

    if square:
        chips = [0, 2, 4, 6]
        to_near = jnp.concatenate([token_columns(bit ^ 1) for bit in chips], axis=1)
        to_keep = jnp.concatenate([token_columns(bit) for bit in chips], axis=1)
        received = swap(mm(to_near, proj_grad, TN).astype(BF16), size, 1)
        kept = (mm(to_keep, proj_grad, TN) + received.astype(F32)).astype(BF16)
        own, for_x, for_y, for_corner = kept.reshape(4, part, columns)
        corner_x, corner_y = swap(for_corner[:half], size, 2), swap(for_corner[half:], size, 4)
        top, low = swap(for_x[:half], size, 2), swap(for_y[half:], size, 4)
        low_x = swap((for_x[half:].astype(F32) + corner_y.astype(F32)).astype(BF16), size, 2)
        top_y = swap((for_y[:half].astype(F32) + corner_x.astype(F32)).astype(BF16), size, 4)
        w_in_grad = jnp.concatenate(
            [
                own[:half].astype(F32) + top.astype(F32) + top_y.astype(F32),
                own[half:].astype(F32) + low.astype(F32) + low_x.astype(F32),
            ]
        )
    else:
        w_in_grad = lax.psum_scatter(
            mm(tokens, proj_grad, TN).astype(BF16), "seq", scatter_dimension=0, tiled=True
        ).astype(F32)
    return (layer_out, input_grad, w_in_grad)


def solution(mesh):
    across = P("seq", "fsdp")
    return jax.shard_map(
        shards,
        mesh=mesh,
        in_specs=(P("seq", None), across, across, across, across),
        out_specs=(across, P("fsdp", "seq"), across),
        check_vma=False,
    )
```

```python
import functools

import jax
import jax.numpy as jnp
from jax import lax
from jax.experimental import pallas as pl
from jax.experimental.pallas import tpu as pltpu
from jax.sharding import PartitionSpec as P

HEAD_DIM = 128
STATE = 128
HEADS = 4
WIDTH = HEADS * HEAD_DIM
STRIP = 128
EXTRA = 16

F32 = jnp.float32
BF16 = jnp.bfloat16
NN = (((1,), (0,)), ((), ()))
NT = (((1,), (1,)), ((), ()))
TN = (((0,), (0,)), ((), ()))


def mm(a, b, dims=NN):
    return lax.dot_general(a, b, dims, preferred_element_type=F32)


def call(kernel, outs, args, flops, place=None):
    scalars = [] if place is None else [place]
    moved = sum(a.size * a.dtype.itemsize for a in (*args, *outs))
    return pl.pallas_call(
        kernel,
        out_shape=outs,
        in_specs=[pl.BlockSpec(memory_space=pltpu.SMEM)] * len(scalars)
        + [pl.BlockSpec(memory_space=pltpu.VMEM)] * len(args),
        out_specs=[pl.BlockSpec(memory_space=pltpu.VMEM)] * len(outs),
        compiler_params=pltpu.CompilerParams(vmem_limit_bytes=40 * 2**20),
        cost_estimate=pl.CostEstimate(flops=flops, bytes_accessed=moved, transcendentals=0),
    )(*scalars, *args)


def head(h):
    return slice(h * HEAD_DIM, (h + 1) * HEAD_DIM)


def split(row, at, ref):
    rest = row
    for k in range(3):
        piece = rest.astype(BF16)
        ref[at + k : at + k + 1, :] = piece
        rest = rest - piece.astype(F32)


def whole(ref, at):
    return sum(ref[at + k : at + k + 1, :].astype(F32) for k in range(3))


def ends_kernel(proj, cot, to_end, growth, total, ends):
    in_map = proj[:, WIDTH : WIDTH + STATE]
    out_map = proj[:, WIDTH + STATE :]
    fed = [
        (proj[:, head(h)].astype(F32) * to_end[:, h : h + 1]).astype(BF16) for h in range(HEADS)
    ]
    grown = [
        (cot[:, head(h)].astype(F32) * growth[:, h : h + 1]).astype(BF16) for h in range(HEADS)
    ]
    ends[:STATE, :] = mm(in_map, jnp.concatenate(fed, axis=1), TN).astype(BF16)
    ends[STATE : 2 * STATE, :] = mm(out_map, jnp.concatenate(grown, axis=1), TN).astype(BF16)
    ends[2 * STATE :, :] = jnp.zeros((EXTRA, WIDTH), BF16)
    split(total[...], 2 * STATE, ends)


def pair_kernel(place, ends, near, for_x, for_y):
    own_total, near_total = whole(ends, 2 * STATE), whole(near, 2 * STATE)
    is_first = place[0] == 0
    one = jnp.ones_like(own_total)
    decay_own, decay_near = jnp.exp(own_total), jnp.exp(near_total)
    forward = ends[:STATE, :].astype(F32) * jnp.where(is_first, decay_near, one) + near[
        :STATE, :
    ].astype(F32) * jnp.where(is_first, one, decay_own)
    backward = ends[STATE : 2 * STATE, :].astype(F32) * jnp.where(is_first, one, decay_near) + near[
        STATE : 2 * STATE, :
    ].astype(F32) * jnp.where(is_first, decay_own, one)
    for out, low in ((for_x, place[1] % 2 == 0), (for_y, place[1] < 2)):
        out[:STATE, :] = jnp.where(low, forward, backward).astype(BF16)
        out[STATE:, :] = jnp.zeros((EXTRA, WIDTH), BF16)
        split(own_total + near_total, STATE, out)


def local_kernel(
    proj, cot, cum, cum_rows, step_rows, to_end, growth, y, dx, db, dc, fed, grown
):
    rows = proj.shape[0]
    for h in range(HEADS):
        fed[:, head(h)] = (proj[:, head(h)].astype(F32) * to_end[:, h : h + 1]).astype(BF16)
        grown[:, head(h)] = (cot[:, head(h)].astype(F32) * growth[:, h : h + 1]).astype(BF16)
    dx[...] = jnp.zeros_like(dx)
    db[...] = jnp.zeros_like(db)
    for at in range(0, rows, STRIP):
        upto = at + STRIP
        here = slice(at, upto)
        in_map = proj[:upto, WIDTH : WIDTH + STATE]
        out_map = proj[here, WIDTH + STATE :]
        scores = mm(out_map, in_map, NT)
        t = lax.broadcasted_iota(jnp.int32, (STRIP, upto), 0) + at
        s = lax.broadcasted_iota(jnp.int32, (STRIP, upto), 1)
        causal = t >= s
        dscores = jnp.zeros_like(scores)
        for h in range(HEADS):
            span = cum[here, h : h + 1] - cum_rows[h : h + 1, :upto]
            factor = jnp.exp(jnp.where(causal, span, -1e30)) * step_rows[h : h + 1, :upto]
            mixing = (scores * factor).astype(BF16)
            values = proj[:upto, head(h)]
            grad = cot[here, head(h)]
            y[here, head(h)] = mm(mixing, values)
            dx[:upto, head(h)] += mm(mixing, grad, TN)
            dscores = dscores + mm(grad, values, NT) * factor
        dscores = dscores.astype(BF16)
        dc[here, :] = mm(dscores, in_map)
        db[:upto, :] += mm(dscores, out_map, TN)


def enter(place, ends, near, far):
    core, chip = place[0], place[1]
    own_total, near_total = whole(ends, 2 * STATE), whole(near, 2 * STATE)
    sums = [own_total + near_total] + [whole(part, STATE) for part in far]
    of_chip = [
        sum(jnp.where((chip ^ bit) == j, sums[bit], 0.0) for bit in range(4)) for j in range(4)
    ]
    decay = jnp.exp(near_total)
    before = jnp.zeros((STATE, WIDTH), F32)
    after = jnp.zeros((STATE, WIDTH), F32)
    for bit in (1, 2, 3):
        there = chip ^ bit
        low, high = jnp.minimum(chip, there), jnp.maximum(chip, there)
        between = sum(jnp.where((j > low) & (j < high), of_chip[j], 0.0) for j in range(4))
        weight = jnp.exp(between)
        value = far[bit - 1][:STATE, :].astype(F32) * weight
        before = before + jnp.where(there < chip, value, 0.0)
        after = after + jnp.where(there > chip, value, 0.0)
    before = jnp.where(core == 1, before * decay + near[:STATE, :].astype(F32), before)
    after = jnp.where(core == 0, after * decay + near[STATE : 2 * STATE, :].astype(F32), after)
    return before.astype(BF16), after.astype(BF16)


def join_kernel(square, place, proj, to_end, dx, db, dc, fed, grown, *rest):
    ends, (proj_grad, turned, entering) = rest[:-3], rest[-3:]
    if square:
        before, after = enter(place, ends[0], ends[1], ends[2:])
    else:
        before, after = ends[0][:STATE, :], ends[0][STATE:, :]
    entering[...] = before
    carried = mm(proj[:, WIDTH : WIDTH + STATE], after)
    for h in range(HEADS):
        proj_grad[:, head(h)] = (dx[:, head(h)] + carried[:, head(h)] * to_end[:, h : h + 1]).astype(BF16)
    proj_grad[:, WIDTH : WIDTH + STATE] = (db[...] + mm(fed[...], after, NT)).astype(BF16)
    proj_grad[:, WIDTH + STATE :] = (dc[...] + mm(grown[...], before, NT)).astype(BF16)
    turned[...] = proj_grad[...].T


def output_kernel(proj, entering, growth, y, out):
    carried = mm(proj[:, WIDTH + STATE :], entering[...])
    for h in range(HEADS):
        out[:, head(h)] = y[:, head(h)] + carried[:, head(h)] * growth[:, h : h + 1]


def swap(value, size, bit):
    return lax.ppermute(value, "seq", [(i, i ^ bit) for i in range(size)])


def once(value, *others):
    return lax.optimization_barrier((value, *others))[0]


def reduce_on_line(weights, grad, group, beside):
    weights = weights.reshape(4, -1, weights.shape[-1])
    low = group < 2

    def product(at):
        return mm(lax.dynamic_index_in_dim(weights, at, 0, keepdims=False), grad)

    def send(value, pairs):
        return lax.ppermute(value.astype(BF16), "fsdp", pairs)

    inward, across, outward = [(0, 1), (3, 2)], [(1, 2), (2, 1)], [(1, 0), (2, 3)]
    far = product(jnp.where(low, 3, 0)).astype(BF16)
    middle = product(jnp.where(low, 2, 1)).astype(BF16)
    near = product(group ^ 1).astype(BF16)
    far_in, middle_in, near_in = send(far, inward), send(middle, inward), send(near, inward)
    beside[0]((far, middle, near))
    far_in = once(far_in, *beside[1]())
    far_across = send(far.astype(F32) + far_in.astype(F32), across)
    middle_in = once(middle_in, *beside[2]())
    middle_across = send(middle.astype(F32) + middle_in.astype(F32), across)
    far_out = send(near.astype(F32) + far_across.astype(F32), outward)
    own = once(product(group), *beside[3]())
    own = own + near_in.astype(F32) + middle_across.astype(F32) + far_out.astype(F32)
    return own.astype(BF16)


def spread(row):
    return jnp.repeat(row, HEAD_DIM, axis=-1)


def shards(tokens, w_in, step_logit, decay_logit, cotangent):
    size = lax.axis_size("seq")
    me = lax.axis_index("seq")
    core, chip = me % 2, me // 2
    square = size == 8
    rows, columns = tokens.shape[0], w_in.shape[1]
    part = w_in.shape[0]
    half = part // 2
    state = jax.ShapeDtypeStruct

    place = jnp.stack([core, chip]).astype(jnp.int32)

    if square:
        from_x, from_y = swap(w_in, size, 2), swap(w_in, size, 4)
        near = swap(w_in, size, 1)
        corner0 = swap(from_x[:half], size, 4)
        corner1 = swap(from_y[half:], size, 2)
        near_x, near_y = swap(from_x, size, 1), swap(from_y, size, 1)
        near0, near1 = swap(corner0, size, 1), swap(corner1, size, 1)
        pieces = [(0, 0, w_in), (1, 0, near), (2, 0, from_x), (4, 0, from_y), (3, 0, near_x), (5, 0, near_y)]
        pieces += [(6, 0, corner0), (6, half, corner1), (7, 0, near0), (7, half, near1)]
        ordered = jnp.concatenate(
            [
                lax.dynamic_slice_in_dim(tokens, (me ^ bit) * part, part, axis=1)
                for bit in (1, 3, 5, 7, 0, 2, 4, 6)
            ],
            axis=1,
        )
        to_near, to_keep = ordered[:, : 4 * part], ordered[:, 4 * part :]
        total = 0.0
        for bit, first, piece in pieces:
            at = (bit // 2 + (0 if bit % 2 else 4)) * part + first
            total = total + mm(ordered[:, at : at + piece.shape[0]], piece)
        projected = total.astype(BF16)
        gathered = jnp.zeros((size, part, columns), BF16)
        for bit, first, piece in pieces:
            gathered = lax.dynamic_update_slice(gathered, piece[None], (me ^ bit, first, 0))
    else:
        gathered = lax.all_gather(w_in, "seq", axis=0, tiled=True)
        projected = mm(tokens, gathered).astype(BF16)
        gathered = gathered.reshape(size, part, columns)

    step_size = jax.nn.softplus(step_logit)
    log_decay = -jax.nn.softplus(decay_logit)
    lower = (
        lax.broadcasted_iota(jnp.int32, (rows, rows), 0) >= lax.broadcasted_iota(jnp.int32, (rows, rows), 1)
    ).astype(F32)
    cum = lax.dot_general(lower, log_decay, NN, precision=lax.Precision.HIGHEST, preferred_element_type=F32)
    log_total = cum[-1]
    growth = jnp.exp(cum)
    to_end = jnp.exp(log_total[None] - cum) * step_size
    cum_rows, step_rows = cum.T, step_size.T
    (ends,) = call(
        ends_kernel,
        [state((2 * STATE + EXTRA, WIDTH), BF16)],
        [projected, cotangent, to_end, growth, spread(log_total)[None]],
        4 * rows * STATE * WIDTH,
    )
    if square:
        near = swap(ends, size, 1)
        for_x, for_y = call(
            pair_kernel, [state((STATE + EXTRA, WIDTH), BF16)] * 2, [ends, near], 0, place
        )
        ends = [ends, near, swap(for_x, size, 2), swap(for_y, size, 4), swap(for_y, size, 6)]
    else:
        everything = lax.all_gather(ends[: 2 * STATE], "seq")
        totals = lax.all_gather(log_total, "seq")
        places = jnp.arange(size)
        until = jnp.stack([jnp.sum(jnp.where((places < k)[:, None], totals, 0.0), axis=0) for k in range(size + 1)])
        reach = jnp.where((places < me)[:, None], until[me][None] - until[1:], -1e30)
        before = jnp.einsum("jnk,jk->nk", everything[:, :STATE].astype(F32), spread(jnp.exp(reach)))
        reach = jnp.where((places > me)[:, None], until[:-1] - until[me + 1][None], -1e30)
        after = jnp.einsum("jnk,jk->nk", everything[:, STATE:].astype(F32), spread(jnp.exp(reach)))
        ends = [jnp.concatenate([before, after]).astype(BF16)]

    y, dx, db, dc, fed, grown = call(
        local_kernel,
        [
            state((rows, WIDTH), F32),
            state((rows, WIDTH), F32),
            state((rows, STATE), F32),
            state((rows, STATE), F32),
            state((rows, WIDTH), BF16),
            state((rows, WIDTH), BF16),
        ],
        [projected, cotangent, cum, cum_rows, step_rows, to_end, growth],
        20 * rows * rows * STATE,
    )
    dx, gathered = lax.optimization_barrier((dx, gathered))
    proj_grad, turned, entering = call(
        functools.partial(join_kernel, square),
        [state((rows, columns), BF16), state((columns, rows), BF16), state((STATE, WIDTH), BF16)],
        [projected, to_end, dx, db, dc, fed, grown, *ends],
        6 * rows * STATE * WIDTH,
        place,
    )
    groups, group = lax.axis_size("fsdp"), lax.axis_index("fsdp")
    kept, sent, out = [], [], []

    def near_products(last):
        products = mm(to_near, once(proj_grad, *last), TN).astype(BF16)
        kept.append(swap(products, size, 1))

    def kept_products():
        kept[0] = (mm(to_keep, proj_grad, TN) + kept[0].astype(F32)).astype(BF16)
        own, for_x, for_y, for_corner = kept[0].reshape(4, part, columns)
        sent.extend((own, for_x, for_y, swap(for_corner[:half], size, 2), swap(for_corner[half:], size, 4)))
        sent.extend((swap(for_x[:half], size, 2), swap(for_y[half:], size, 4)))
        return (kept[0],)

    def corner_sums():
        own, for_x, for_y, corner_x, corner_y, top, low = sent
        last_x = (for_x[half:].astype(F32) + corner_y.astype(F32)).astype(BF16)
        last_y = (for_y[:half].astype(F32) + corner_x.astype(F32)).astype(BF16)
        sent.extend((swap(last_x, size, 2), swap(last_y, size, 4)))
        return last_x, last_y

    def outputs():
        out.extend(
            call(
                output_kernel,
                [state((rows, WIDTH), F32)],
                [projected, entering, growth, y],
                2 * rows * STATE * WIDTH,
            )
        )
        return tuple(out)

    if square and groups == 4:
        input_grad = reduce_on_line(gathered, turned, group, (near_products, kept_products, corner_sums, outputs))
    else:
        input_grad = lax.psum_scatter(
            mm(gathered.reshape(part * size, columns), turned).astype(BF16), "fsdp", scatter_dimension=0, tiled=True
        )
        outputs()
    (layer_out,) = out

    if square and groups == 4:
        own, for_x, for_y, corner_x, corner_y, top, low, low_x, top_y = sent
        w_in_grad = jnp.concatenate(
            [
                own[:half].astype(F32) + top.astype(F32) + top_y.astype(F32),
                own[half:].astype(F32) + low.astype(F32) + low_x.astype(F32),
            ]
        )
    else:
        w_in_grad = lax.psum_scatter(
            mm(tokens, proj_grad, TN).astype(BF16), "seq", scatter_dimension=0, tiled=True
        ).astype(F32)
    return (layer_out, input_grad, w_in_grad)


def solution(mesh):
    across = P("seq", "fsdp")
    return jax.shard_map(
        shards,
        mesh=mesh,
        in_specs=(P("seq", None), across, across, across, across),
        out_specs=(across, P("fsdp", "seq"), across),
        check_vma=False,
    )
```

```python
import functools

import jax
import jax.numpy as jnp
from jax import lax
from jax.experimental import pallas as pl
from jax.experimental.pallas import tpu as pltpu
from jax.sharding import PartitionSpec as P

HEAD_DIM = 128
STATE = 128
HEADS = 4
WIDTH = HEADS * HEAD_DIM
STRIP = 128
EXTRA = 16

F32 = jnp.float32
BF16 = jnp.bfloat16
NN = (((1,), (0,)), ((), ()))
NT = (((1,), (1,)), ((), ()))
TN = (((0,), (0,)), ((), ()))


def mm(a, b, dims=NN):
    return lax.dot_general(a, b, dims, preferred_element_type=F32)


def call(kernel, outs, args, flops, place=None):
    scalars = [] if place is None else [place]
    moved = sum(a.size * a.dtype.itemsize for a in (*args, *outs))
    return pl.pallas_call(
        kernel,
        out_shape=outs,
        in_specs=[pl.BlockSpec(memory_space=pltpu.SMEM)] * len(scalars)
        + [pl.BlockSpec(memory_space=pltpu.VMEM)] * len(args),
        out_specs=[pl.BlockSpec(memory_space=pltpu.VMEM)] * len(outs),
        compiler_params=pltpu.CompilerParams(vmem_limit_bytes=40 * 2**20),
        cost_estimate=pl.CostEstimate(flops=flops, bytes_accessed=moved, transcendentals=0),
    )(*scalars, *args)


def head(h):
    return slice(h * HEAD_DIM, (h + 1) * HEAD_DIM)


def split(row, at, ref):
    rest = row
    for k in range(3):
        piece = rest.astype(BF16)
        ref[at + k : at + k + 1, :] = piece
        rest = rest - piece.astype(F32)


def whole(ref, at):
    return sum(ref[at + k : at + k + 1, :].astype(F32) for k in range(3))


def ends_kernel(proj, cot, to_end, growth, total, ends):
    in_map = proj[:, WIDTH : WIDTH + STATE]
    out_map = proj[:, WIDTH + STATE :]
    fed = [
        (proj[:, head(h)].astype(F32) * to_end[:, h : h + 1]).astype(BF16) for h in range(HEADS)
    ]
    grown = [
        (cot[:, head(h)].astype(F32) * growth[:, h : h + 1]).astype(BF16) for h in range(HEADS)
    ]
    ends[:STATE, :] = mm(in_map, jnp.concatenate(fed, axis=1), TN).astype(BF16)
    ends[STATE : 2 * STATE, :] = mm(out_map, jnp.concatenate(grown, axis=1), TN).astype(BF16)
    ends[2 * STATE :, :] = jnp.zeros((EXTRA, WIDTH), BF16)
    split(total[...], 2 * STATE, ends)


def pair_kernel(place, ends, near, for_x, for_y):
    own_total, near_total = whole(ends, 2 * STATE), whole(near, 2 * STATE)
    is_first = place[0] == 0
    one = jnp.ones_like(own_total)
    decay_own, decay_near = jnp.exp(own_total), jnp.exp(near_total)
    forward = ends[:STATE, :].astype(F32) * jnp.where(is_first, decay_near, one) + near[
        :STATE, :
    ].astype(F32) * jnp.where(is_first, one, decay_own)
    backward = ends[STATE : 2 * STATE, :].astype(F32) * jnp.where(is_first, one, decay_near) + near[
        STATE : 2 * STATE, :
    ].astype(F32) * jnp.where(is_first, decay_own, one)
    for out, low in ((for_x, place[1] % 2 == 0), (for_y, place[1] < 2)):
        out[:STATE, :] = jnp.where(low, forward, backward).astype(BF16)
        out[STATE:, :] = jnp.zeros((EXTRA, WIDTH), BF16)
        split(own_total + near_total, STATE, out)


def local_kernel(
    proj, cot, cum, cum_rows, step_rows, to_end, growth, y, dx, db, dc, fed, grown
):
    rows = proj.shape[0]
    for h in range(HEADS):
        fed[:, head(h)] = (proj[:, head(h)].astype(F32) * to_end[:, h : h + 1]).astype(BF16)
        grown[:, head(h)] = (cot[:, head(h)].astype(F32) * growth[:, h : h + 1]).astype(BF16)
    dx[...] = jnp.zeros_like(dx)
    db[...] = jnp.zeros_like(db)
    for at in range(0, rows, STRIP):
        upto = at + STRIP
        here = slice(at, upto)
        in_map = proj[:upto, WIDTH : WIDTH + STATE]
        out_map = proj[here, WIDTH + STATE :]
        scores = mm(out_map, in_map, NT)
        t = lax.broadcasted_iota(jnp.int32, (STRIP, upto), 0) + at
        s = lax.broadcasted_iota(jnp.int32, (STRIP, upto), 1)
        causal = t >= s
        dscores = jnp.zeros_like(scores)
        for h in range(HEADS):
            span = cum[here, h : h + 1] - cum_rows[h : h + 1, :upto]
            factor = jnp.exp(jnp.where(causal, span, -1e30)) * step_rows[h : h + 1, :upto]
            mixing = (scores * factor).astype(BF16)
            values = proj[:upto, head(h)]
            grad = cot[here, head(h)]
            y[here, head(h)] = mm(mixing, values)
            dx[:upto, head(h)] += mm(mixing, grad, TN)
            dscores = dscores + mm(grad, values, NT) * factor
        dscores = dscores.astype(BF16)
        dc[here, :] = mm(dscores, in_map)
        db[:upto, :] += mm(dscores, out_map, TN)


def enter(place, ends, near, far):
    core, chip = place[0], place[1]
    own_total, near_total = whole(ends, 2 * STATE), whole(near, 2 * STATE)
    sums = [own_total + near_total] + [whole(part, STATE) for part in far]
    of_chip = [
        sum(jnp.where((chip ^ bit) == j, sums[bit], 0.0) for bit in range(4)) for j in range(4)
    ]
    decay = jnp.exp(near_total)
    before = jnp.zeros((STATE, WIDTH), F32)
    after = jnp.zeros((STATE, WIDTH), F32)
    for bit in (1, 2, 3):
        there = chip ^ bit
        low, high = jnp.minimum(chip, there), jnp.maximum(chip, there)
        between = sum(jnp.where((j > low) & (j < high), of_chip[j], 0.0) for j in range(4))
        weight = jnp.exp(between)
        value = far[bit - 1][:STATE, :].astype(F32) * weight
        before = before + jnp.where(there < chip, value, 0.0)
        after = after + jnp.where(there > chip, value, 0.0)
    before = jnp.where(core == 1, before * decay + near[:STATE, :].astype(F32), before)
    after = jnp.where(core == 0, after * decay + near[STATE : 2 * STATE, :].astype(F32), after)
    return before.astype(BF16), after.astype(BF16)


def join_kernel(square, place, proj, to_end, dx, db, dc, fed, grown, *rest):
    ends, (proj_grad, turned, entering) = rest[:-3], rest[-3:]
    if square:
        before, after = enter(place, ends[0], ends[1], ends[2:])
    else:
        before, after = ends[0][:STATE, :], ends[0][STATE:, :]
    entering[...] = before
    carried = mm(proj[:, WIDTH : WIDTH + STATE], after)
    for h in range(HEADS):
        proj_grad[:, head(h)] = (dx[:, head(h)] + carried[:, head(h)] * to_end[:, h : h + 1]).astype(BF16)
    proj_grad[:, WIDTH : WIDTH + STATE] = (db[...] + mm(fed[...], after, NT)).astype(BF16)
    proj_grad[:, WIDTH + STATE :] = (dc[...] + mm(grown[...], before, NT)).astype(BF16)
    turned[...] = proj_grad[...].T


def output_kernel(proj, entering, growth, y, out):
    carried = mm(proj[:, WIDTH + STATE :], entering[...])
    for h in range(HEADS):
        out[:, head(h)] = y[:, head(h)] + carried[:, head(h)] * growth[:, h : h + 1]


def swap(value, size, bit):
    return lax.ppermute(value, "seq", [(i, i ^ bit) for i in range(size)])


def once(value, *others):
    return lax.optimization_barrier((value, *others))[0]


def reduce_on_line(weights, grad, group, beside):
    weights = weights.reshape(4, -1, weights.shape[-1])
    low = group < 2

    def product(at):
        return mm(lax.dynamic_index_in_dim(weights, at, 0, keepdims=False), grad)

    def send(value, pairs):
        return lax.ppermute(value.astype(BF16), "fsdp", pairs)

    inward, across, outward = [(0, 1), (3, 2)], [(1, 2), (2, 1)], [(1, 0), (2, 3)]
    far = product(jnp.where(low, 3, 0)).astype(BF16)
    middle = product(jnp.where(low, 2, 1)).astype(BF16)
    near = product(group ^ 1).astype(BF16)
    far_in, middle_in, near_in = send(far, inward), send(middle, inward), send(near, inward)
    beside[0]((far, middle, near))
    far_in = once(far_in, *beside[1]())
    far_across = send(far.astype(F32) + far_in.astype(F32), across)
    middle_in = once(middle_in, *beside[2]())
    middle_across = send(middle.astype(F32) + middle_in.astype(F32), across)
    far_out = send(near.astype(F32) + far_across.astype(F32), outward)
    own = once(product(group), *beside[3]())
    own, near_in, middle_across, far_out = lax.optimization_barrier((own, near_in, middle_across, far_out))
    return (own + near_in.astype(F32) + middle_across.astype(F32) + far_out.astype(F32)).astype(BF16)


def spread(row):
    return jnp.repeat(row, HEAD_DIM, axis=-1)


def shards(tokens, w_in, step_logit, decay_logit, cotangent):
    size = lax.axis_size("seq")
    me = lax.axis_index("seq")
    core, chip = me % 2, me // 2
    square = size == 8
    rows, columns = tokens.shape[0], w_in.shape[1]
    part = w_in.shape[0]
    half = part // 2
    state = jax.ShapeDtypeStruct

    place = jnp.stack([core, chip]).astype(jnp.int32)

    if square:
        from_x, from_y = swap(w_in, size, 2), swap(w_in, size, 4)
        near = swap(w_in, size, 1)
        corner = jnp.concatenate([swap(from_x[:half], size, 4), swap(from_y[half:], size, 2)])
        near_x, near_y, near_corner = swap(from_x, size, 1), swap(from_y, size, 1), swap(corner, size, 1)
        pieces = [(0, w_in), (1, near), (2, from_x), (4, from_y), (3, near_x), (5, near_y)]
        pieces += [(6, corner), (7, near_corner)]
        ordered = jnp.concatenate(
            [
                lax.dynamic_slice_in_dim(tokens, (me ^ bit) * part, part, axis=1)
                for bit in (1, 3, 5, 7, 0, 2, 4, 6)
            ],
            axis=1,
        )
        to_near, to_keep = ordered[:, : 4 * part], ordered[:, 4 * part :]
        total = 0.0
        for bit, piece in pieces:
            at = (bit // 2 + (0 if bit % 2 else 4)) * part
            total = total + mm(ordered[:, at : at + part], piece)
        projected = total.astype(BF16)
        gathered = jnp.zeros((size, part, columns), BF16)
        for bit, piece in pieces:
            gathered = lax.dynamic_update_slice(gathered, piece[None], (me ^ bit, 0, 0))
    else:
        gathered = lax.all_gather(w_in, "seq", axis=0, tiled=True)
        projected = mm(tokens, gathered).astype(BF16)
        gathered = gathered.reshape(size, part, columns)

    step_size = jax.nn.softplus(step_logit)
    log_decay = -jax.nn.softplus(decay_logit)
    lower = (
        lax.broadcasted_iota(jnp.int32, (rows, rows), 0) >= lax.broadcasted_iota(jnp.int32, (rows, rows), 1)
    ).astype(F32)
    cum = lax.dot_general(lower, log_decay, NN, precision=lax.Precision.HIGHEST, preferred_element_type=F32)
    log_total = cum[-1]
    growth = jnp.exp(cum)
    to_end = jnp.exp(log_total[None] - cum) * step_size
    cum_rows, step_rows = cum.T, step_size.T
    (ends,) = call(
        ends_kernel,
        [state((2 * STATE + EXTRA, WIDTH), BF16)],
        [projected, cotangent, to_end, growth, spread(log_total)[None]],
        4 * rows * STATE * WIDTH,
    )
    if square:
        near = swap(ends, size, 1)
        for_x, for_y = call(
            pair_kernel, [state((STATE + EXTRA, WIDTH), BF16)] * 2, [ends, near], 0, place
        )
        ends = [ends, near, swap(for_x, size, 2), swap(for_y, size, 4), swap(for_y, size, 6)]
    else:
        everything = lax.all_gather(ends[: 2 * STATE], "seq")
        totals = lax.all_gather(log_total, "seq")
        places = jnp.arange(size)
        until = jnp.stack([jnp.sum(jnp.where((places < k)[:, None], totals, 0.0), axis=0) for k in range(size + 1)])
        reach = jnp.where((places < me)[:, None], until[me][None] - until[1:], -1e30)
        before = jnp.einsum("jnk,jk->nk", everything[:, :STATE].astype(F32), spread(jnp.exp(reach)))
        reach = jnp.where((places > me)[:, None], until[:-1] - until[me + 1][None], -1e30)
        after = jnp.einsum("jnk,jk->nk", everything[:, STATE:].astype(F32), spread(jnp.exp(reach)))
        ends = [jnp.concatenate([before, after]).astype(BF16)]

    y, dx, db, dc, fed, grown = call(
        local_kernel,
        [
            state((rows, WIDTH), F32),
            state((rows, WIDTH), F32),
            state((rows, STATE), F32),
            state((rows, STATE), F32),
            state((rows, WIDTH), BF16),
            state((rows, WIDTH), BF16),
        ],
        [projected, cotangent, cum, cum_rows, step_rows, to_end, growth],
        20 * rows * rows * STATE,
    )
    dx, gathered = lax.optimization_barrier((dx, gathered))
    proj_grad, turned, entering = call(
        functools.partial(join_kernel, square),
        [state((rows, columns), BF16), state((columns, rows), BF16), state((STATE, WIDTH), BF16)],
        [projected, to_end, dx, db, dc, fed, grown, *ends],
        6 * rows * STATE * WIDTH,
        place,
    )
    groups, group = lax.axis_size("fsdp"), lax.axis_index("fsdp")
    kept, sent, out = [], [], []

    def near_products(last):
        products = mm(to_near, once(proj_grad, *last), TN).astype(BF16)
        kept.append(swap(products, size, 1))

    def kept_products():
        kept[0] = (mm(to_keep, proj_grad, TN) + kept[0].astype(F32)).astype(BF16)
        own, for_x, for_y, for_corner = kept[0].reshape(4, part, columns)
        sent.extend((own, for_x, for_y, swap(for_corner[:half], size, 2), swap(for_corner[half:], size, 4)))
        sent.extend((swap(for_x[:half], size, 2), swap(for_y[half:], size, 4)))
        return (kept[0],)

    def corner_sums():
        own, for_x, for_y, corner_x, corner_y, top, low = sent
        last_x = (for_x[half:].astype(F32) + corner_y.astype(F32)).astype(BF16)
        last_y = (for_y[:half].astype(F32) + corner_x.astype(F32)).astype(BF16)
        sent.extend((swap(last_x, size, 2), swap(last_y, size, 4)))
        return last_x, last_y

    def outputs():
        out.extend(
            call(
                output_kernel,
                [state((rows, WIDTH), F32)],
                [projected, entering, growth, y],
                2 * rows * STATE * WIDTH,
            )
        )
        return tuple(out)

    if square and groups == 4:
        input_grad = reduce_on_line(gathered, turned, group, (near_products, kept_products, corner_sums, outputs))
    else:
        input_grad = lax.psum_scatter(
            mm(gathered.reshape(part * size, columns), turned).astype(BF16), "fsdp", scatter_dimension=0, tiled=True
        )
        outputs()
    (layer_out,) = out

    if square and groups == 4:
        own, for_x, for_y, corner_x, corner_y, top, low, low_x, top_y = sent
        w_in_grad = jnp.concatenate(
            [
                own[:half].astype(F32) + top.astype(F32) + top_y.astype(F32),
                own[half:].astype(F32) + low.astype(F32) + low_x.astype(F32),
            ]
        )
    else:
        w_in_grad = lax.psum_scatter(
            mm(tokens, proj_grad, TN).astype(BF16), "seq", scatter_dimension=0, tiled=True
        ).astype(F32)
    return (layer_out, input_grad, w_in_grad)


def solution(mesh):
    across = P("seq", "fsdp")
    return jax.shard_map(
        shards,
        mesh=mesh,
        in_specs=(P("seq", None), across, across, across, across),
        out_specs=(across, P("fsdp", "seq"), across),
        check_vma=False,
    )
```

```python
import functools

import jax
import jax.numpy as jnp
from jax import lax
from jax.experimental import pallas as pl
from jax.experimental.pallas import tpu as pltpu
from jax.sharding import PartitionSpec as P

HEAD_DIM = 128
STATE = 128
HEADS = 4
WIDTH = HEADS * HEAD_DIM
STRIP = 128
EXTRA = 16

F32 = jnp.float32
BF16 = jnp.bfloat16
NN = (((1,), (0,)), ((), ()))
NT = (((1,), (1,)), ((), ()))
TN = (((0,), (0,)), ((), ()))


def mm(a, b, dims=NN):
    return lax.dot_general(a, b, dims, preferred_element_type=F32)


def call(kernel, outs, args, flops, place=None):
    scalars = [] if place is None else [place]
    moved = sum(a.size * a.dtype.itemsize for a in (*args, *outs))
    return pl.pallas_call(
        kernel,
        out_shape=outs,
        in_specs=[pl.BlockSpec(memory_space=pltpu.SMEM)] * len(scalars)
        + [pl.BlockSpec(memory_space=pltpu.VMEM)] * len(args),
        out_specs=[pl.BlockSpec(memory_space=pltpu.VMEM)] * len(outs),
        compiler_params=pltpu.CompilerParams(vmem_limit_bytes=14 * 2**20),
        cost_estimate=pl.CostEstimate(flops=flops, bytes_accessed=moved, transcendentals=0),
    )(*scalars, *args)


def head(h):
    return slice(h * HEAD_DIM, (h + 1) * HEAD_DIM)


def split(row, at, ref):
    rest = row
    for k in range(3):
        piece = rest.astype(BF16)
        ref[at + k : at + k + 1, :] = piece
        rest = rest - piece.astype(F32)


def whole(ref, at):
    return sum(ref[at + k : at + k + 1, :].astype(F32) for k in range(3))


def ends_kernel(proj, cot, to_end, growth, total, ends):
    in_map = proj[:, WIDTH : WIDTH + STATE]
    out_map = proj[:, WIDTH + STATE :]
    fed = [
        (proj[:, head(h)].astype(F32) * to_end[:, h : h + 1]).astype(BF16) for h in range(HEADS)
    ]
    grown = [
        (cot[:, head(h)].astype(F32) * growth[:, h : h + 1]).astype(BF16) for h in range(HEADS)
    ]
    ends[:STATE, :] = mm(in_map, jnp.concatenate(fed, axis=1), TN).astype(BF16)
    ends[STATE : 2 * STATE, :] = mm(out_map, jnp.concatenate(grown, axis=1), TN).astype(BF16)
    ends[2 * STATE :, :] = jnp.zeros((EXTRA, WIDTH), BF16)
    split(total[...], 2 * STATE, ends)


def pair_kernel(place, ends, near, for_x, for_y):
    own_total, near_total = whole(ends, 2 * STATE), whole(near, 2 * STATE)
    is_first = place[0] == 0
    one = jnp.ones_like(own_total)
    decay_own, decay_near = jnp.exp(own_total), jnp.exp(near_total)
    forward = ends[:STATE, :].astype(F32) * jnp.where(is_first, decay_near, one) + near[
        :STATE, :
    ].astype(F32) * jnp.where(is_first, one, decay_own)
    backward = ends[STATE : 2 * STATE, :].astype(F32) * jnp.where(is_first, one, decay_near) + near[
        STATE : 2 * STATE, :
    ].astype(F32) * jnp.where(is_first, decay_own, one)
    for out, low in ((for_x, place[1] % 2 == 0), (for_y, place[1] < 2)):
        out[:STATE, :] = jnp.where(low, forward, backward).astype(BF16)
        out[STATE:, :] = jnp.zeros((EXTRA, WIDTH), BF16)
        split(own_total + near_total, STATE, out)


def local_kernel(
    proj, cot, cum, cum_rows, step_rows, to_end, growth, y, dx, db, dc, fed, grown
):
    rows = proj.shape[0]
    for h in range(HEADS):
        fed[:, head(h)] = (proj[:, head(h)].astype(F32) * to_end[:, h : h + 1]).astype(BF16)
        grown[:, head(h)] = (cot[:, head(h)].astype(F32) * growth[:, h : h + 1]).astype(BF16)
    dx[...] = jnp.zeros_like(dx)
    db[...] = jnp.zeros_like(db)
    for at in range(0, rows, STRIP):
        upto = at + STRIP
        here = slice(at, upto)
        in_map = proj[:upto, WIDTH : WIDTH + STATE]
        out_map = proj[here, WIDTH + STATE :]
        scores = mm(out_map, in_map, NT)
        t = lax.broadcasted_iota(jnp.int32, (STRIP, upto), 0) + at
        s = lax.broadcasted_iota(jnp.int32, (STRIP, upto), 1)
        causal = t >= s
        dscores = jnp.zeros_like(scores)
        for h in range(HEADS):
            span = cum[here, h : h + 1] - cum_rows[h : h + 1, :upto]
            factor = jnp.exp(jnp.where(causal, span, -1e30)) * step_rows[h : h + 1, :upto]
            mixing = (scores * factor).astype(BF16)
            values = proj[:upto, head(h)]
            grad = cot[here, head(h)]
            y[here, head(h)] = mm(mixing, values)
            dx[:upto, head(h)] += mm(mixing, grad, TN)
            dscores = dscores + mm(grad, values, NT) * factor
        dscores = dscores.astype(BF16)
        dc[here, :] = mm(dscores, in_map)
        db[:upto, :] += mm(dscores, out_map, TN)


def enter(place, ends, near, far):
    core, chip = place[0], place[1]
    own_total, near_total = whole(ends, 2 * STATE), whole(near, 2 * STATE)
    sums = [own_total + near_total] + [whole(part, STATE) for part in far]
    of_chip = [
        sum(jnp.where((chip ^ bit) == j, sums[bit], 0.0) for bit in range(4)) for j in range(4)
    ]
    decay = jnp.exp(near_total)
    before = jnp.zeros((STATE, WIDTH), F32)
    after = jnp.zeros((STATE, WIDTH), F32)
    for bit in (1, 2, 3):
        there = chip ^ bit
        low, high = jnp.minimum(chip, there), jnp.maximum(chip, there)
        between = sum(jnp.where((j > low) & (j < high), of_chip[j], 0.0) for j in range(4))
        weight = jnp.exp(between)
        value = far[bit - 1][:STATE, :].astype(F32) * weight
        before = before + jnp.where(there < chip, value, 0.0)
        after = after + jnp.where(there > chip, value, 0.0)
    before = jnp.where(core == 1, before * decay + near[:STATE, :].astype(F32), before)
    after = jnp.where(core == 0, after * decay + near[STATE : 2 * STATE, :].astype(F32), after)
    return before.astype(BF16), after.astype(BF16)


def join_kernel(square, place, proj, to_end, dx, db, dc, fed, grown, *rest):
    ends, (proj_grad, turned, entering) = rest[:-3], rest[-3:]
    if square:
        before, after = enter(place, ends[0], ends[1], ends[2:])
    else:
        before, after = ends[0][:STATE, :], ends[0][STATE:, :]
    entering[...] = before
    carried = mm(proj[:, WIDTH : WIDTH + STATE], after)
    for h in range(HEADS):
        proj_grad[:, head(h)] = (dx[:, head(h)] + carried[:, head(h)] * to_end[:, h : h + 1]).astype(BF16)
    proj_grad[:, WIDTH : WIDTH + STATE] = (db[...] + mm(fed[...], after, NT)).astype(BF16)
    proj_grad[:, WIDTH + STATE :] = (dc[...] + mm(grown[...], before, NT)).astype(BF16)
    turned[...] = proj_grad[...].T


def output_kernel(proj, entering, growth, y, out):
    carried = mm(proj[:, WIDTH + STATE :], entering[...])
    for h in range(HEADS):
        out[:, head(h)] = y[:, head(h)] + carried[:, head(h)] * growth[:, h : h + 1]


def swap(value, size, bit):
    return lax.ppermute(value, "seq", [(i, i ^ bit) for i in range(size)])


def once(value, *others):
    return lax.optimization_barrier((value, *others))[0]


def reduce_on_line(weights, grad, group, beside):
    weights = weights.reshape(4, -1, weights.shape[-1])
    low = group < 2

    def product(at):
        return mm(lax.dynamic_index_in_dim(weights, at, 0, keepdims=False), grad)

    def send(value, pairs):
        return lax.ppermute(value.astype(BF16), "fsdp", pairs)

    inward, across, outward = [(0, 1), (3, 2)], [(1, 2), (2, 1)], [(1, 0), (2, 3)]
    far = product(jnp.where(low, 3, 0)).astype(BF16)
    middle = product(jnp.where(low, 2, 1)).astype(BF16)
    near = product(group ^ 1).astype(BF16)
    far_in, middle_in, near_in = send(far, inward), send(middle, inward), send(near, inward)
    beside[0]((far, middle, near))
    far_in = once(far_in, *beside[1]())
    far_across = send(far.astype(F32) + far_in.astype(F32), across)
    middle_in = once(middle_in, *beside[2]())
    middle_across = send(middle.astype(F32) + middle_in.astype(F32), across)
    far_out = send(near.astype(F32) + far_across.astype(F32), outward)
    own = once(product(group), *beside[3]())
    own, near_in, middle_across, far_out = lax.optimization_barrier((own, near_in, middle_across, far_out))
    return (own + near_in.astype(F32) + middle_across.astype(F32) + far_out.astype(F32)).astype(BF16)


def spread(row):
    return jnp.repeat(row, HEAD_DIM, axis=-1)


def shards(tokens, w_in, step_logit, decay_logit, cotangent):
    size = lax.axis_size("seq")
    me = lax.axis_index("seq")
    core, chip = me % 2, me // 2
    square = size == 8
    rows, columns = tokens.shape[0], w_in.shape[1]
    part = w_in.shape[0]
    half = part // 2
    state = jax.ShapeDtypeStruct

    place = jnp.stack([core, chip]).astype(jnp.int32)

    if square:
        from_x, from_y = swap(w_in, size, 2), swap(w_in, size, 4)
        near = swap(w_in, size, 1)
        corner = jnp.concatenate([swap(from_x[:half], size, 4), swap(from_y[half:], size, 2)])
        near_x, near_y, near_corner = swap(from_x, size, 1), swap(from_y, size, 1), swap(corner, size, 1)
        pieces = [(0, w_in), (1, near), (2, from_x), (4, from_y), (3, near_x), (5, near_y)]
        pieces += [(6, corner), (7, near_corner)]
        ordered = jnp.concatenate(
            [
                lax.dynamic_slice_in_dim(tokens, (me ^ bit) * part, part, axis=1)
                for bit in (1, 3, 5, 7, 0, 2, 4, 6)
            ],
            axis=1,
        )
        to_near, to_keep = ordered[:, : 4 * part], ordered[:, 4 * part :]
        chip_tokens = jnp.concatenate([to_keep, swap(to_near, size, 1)])
        total = 0.0
        for bit, piece in pieces:
            at = (bit // 2 + (0 if bit % 2 else 4)) * part
            total = total + mm(ordered[:, at : at + part], piece)
        projected = total.astype(BF16)
        gathered = jnp.zeros((size, part, columns), BF16)
        for bit, piece in pieces:
            gathered = lax.dynamic_update_slice(gathered, piece[None], (me ^ bit, 0, 0))
    else:
        gathered = lax.all_gather(w_in, "seq", axis=0, tiled=True)
        projected = mm(tokens, gathered).astype(BF16)
        gathered = gathered.reshape(size, part, columns)

    step_size = jax.nn.softplus(step_logit)
    log_decay = -jax.nn.softplus(decay_logit)
    lower = (
        lax.broadcasted_iota(jnp.int32, (rows, rows), 0) >= lax.broadcasted_iota(jnp.int32, (rows, rows), 1)
    ).astype(F32)
    cum = lax.dot_general(lower, log_decay, NN, precision=lax.Precision.HIGHEST, preferred_element_type=F32)
    log_total = cum[-1]
    growth = jnp.exp(cum)
    to_end = jnp.exp(log_total[None] - cum) * step_size
    cum_rows, step_rows = cum.T, step_size.T
    (ends,) = call(
        ends_kernel,
        [state((2 * STATE + EXTRA, WIDTH), BF16)],
        [projected, cotangent, to_end, growth, spread(log_total)[None]],
        4 * rows * STATE * WIDTH,
    )
    if square:
        near = swap(ends, size, 1)
        for_x, for_y = call(
            pair_kernel, [state((STATE + EXTRA, WIDTH), BF16)] * 2, [ends, near], 0, place
        )
        ends = [ends, near, swap(for_x, size, 2), swap(for_y, size, 4), swap(for_y, size, 6)]
    else:
        everything = lax.all_gather(ends[: 2 * STATE], "seq")
        totals = lax.all_gather(log_total, "seq")
        places = jnp.arange(size)
        until = jnp.stack([jnp.sum(jnp.where((places < k)[:, None], totals, 0.0), axis=0) for k in range(size + 1)])
        reach = jnp.where((places < me)[:, None], until[me][None] - until[1:], -1e30)
        before = jnp.einsum("jnk,jk->nk", everything[:, :STATE].astype(F32), spread(jnp.exp(reach)))
        reach = jnp.where((places > me)[:, None], until[:-1] - until[me + 1][None], -1e30)
        after = jnp.einsum("jnk,jk->nk", everything[:, STATE:].astype(F32), spread(jnp.exp(reach)))
        ends = [jnp.concatenate([before, after]).astype(BF16)]

    y, dx, db, dc, fed, grown = call(
        local_kernel,
        [
            state((rows, WIDTH), F32),
            state((rows, WIDTH), F32),
            state((rows, STATE), F32),
            state((rows, STATE), F32),
            state((rows, WIDTH), BF16),
            state((rows, WIDTH), BF16),
        ],
        [projected, cotangent, cum, cum_rows, step_rows, to_end, growth],
        20 * rows * rows * STATE,
    )
    dx, gathered = lax.optimization_barrier((dx, gathered))
    proj_grad, turned, entering = call(
        functools.partial(join_kernel, square),
        [state((rows, columns), BF16), state((columns, rows), BF16), state((STATE, WIDTH), BF16)],
        [projected, to_end, dx, db, dc, fed, grown, *ends],
        6 * rows * STATE * WIDTH,
        place,
    )
    groups, group = lax.axis_size("fsdp"), lax.axis_index("fsdp")
    kept, sent, out = [], [], []

    def near_gradient(last):
        kept.append(swap(proj_grad, size, 1))

    def kept_products():
        kept[0] = mm(chip_tokens, jnp.concatenate([proj_grad, kept[0]]), TN).astype(BF16)
        own, for_x, for_y, for_corner = kept[0].reshape(4, part, columns)
        sent.extend((own, for_x, for_y, swap(for_corner[:half], size, 2), swap(for_corner[half:], size, 4)))
        sent.extend((swap(for_x[:half], size, 2), swap(for_y[half:], size, 4)))
        return (kept[0],)

    def corner_sums():
        own, for_x, for_y, corner_x, corner_y, top, low = sent
        last_x = (for_x[half:].astype(F32) + corner_y.astype(F32)).astype(BF16)
        last_y = (for_y[:half].astype(F32) + corner_x.astype(F32)).astype(BF16)
        sent.extend((swap(last_x, size, 2), swap(last_y, size, 4)))
        return last_x, last_y

    def outputs():
        out.extend(
            call(
                output_kernel,
                [state((rows, WIDTH), F32)],
                [projected, entering, growth, y],
                2 * rows * STATE * WIDTH,
            )
        )
        return tuple(out)

    if square and groups == 4:
        input_grad = reduce_on_line(gathered, turned, group, (near_gradient, kept_products, corner_sums, outputs))
    else:
        input_grad = lax.psum_scatter(
            mm(gathered.reshape(part * size, columns), turned).astype(BF16), "fsdp", scatter_dimension=0, tiled=True
        )
        outputs()
    (layer_out,) = out

    if square and groups == 4:
        own, for_x, for_y, corner_x, corner_y, top, low, low_x, top_y = sent
        w_in_grad = jnp.concatenate(
            [
                own[:half].astype(F32) + top.astype(F32) + top_y.astype(F32),
                own[half:].astype(F32) + low.astype(F32) + low_x.astype(F32),
            ]
        )
    else:
        w_in_grad = lax.psum_scatter(
            mm(tokens, proj_grad, TN).astype(BF16), "seq", scatter_dimension=0, tiled=True
        ).astype(F32)
    return (layer_out, input_grad, w_in_grad)


def solution(mesh):
    across = P("seq", "fsdp")
    return jax.shard_map(
        shards,
        mesh=mesh,
        in_specs=(P("seq", None), across, across, across, across),
        out_specs=(across, P("fsdp", "seq"), across),
        check_vma=False,
    )
```

```python
import functools

import jax
import jax.numpy as jnp
from jax import lax
from jax.experimental import pallas as pl
from jax.experimental.pallas import tpu as pltpu
from jax.sharding import PartitionSpec as P

HEAD_DIM = 128
STATE = 128
HEADS = 4
WIDTH = HEADS * HEAD_DIM
STRIP = 128
EXTRA = 16

F32 = jnp.float32
BF16 = jnp.bfloat16
NN = (((1,), (0,)), ((), ()))
NT = (((1,), (1,)), ((), ()))
TN = (((0,), (0,)), ((), ()))


def mm(a, b, dims=NN):
    return lax.dot_general(a, b, dims, preferred_element_type=F32)


def call(kernel, outs, args, flops, place=None):
    scalars = [] if place is None else [place]
    moved = sum(a.size * a.dtype.itemsize for a in (*args, *outs))
    return pl.pallas_call(
        kernel,
        out_shape=outs,
        in_specs=[pl.BlockSpec(memory_space=pltpu.SMEM)] * len(scalars)
        + [pl.BlockSpec(memory_space=pltpu.VMEM)] * len(args),
        out_specs=[pl.BlockSpec(memory_space=pltpu.VMEM)] * len(outs),
        compiler_params=pltpu.CompilerParams(vmem_limit_bytes=40 * 2**20),
        cost_estimate=pl.CostEstimate(flops=flops, bytes_accessed=moved, transcendentals=0),
    )(*scalars, *args)


def head(h):
    return slice(h * HEAD_DIM, (h + 1) * HEAD_DIM)


def split(row, at, ref):
    rest = row
    for k in range(3):
        piece = rest.astype(BF16)
        ref[at + k : at + k + 1, :] = piece
        rest = rest - piece.astype(F32)


def whole(ref, at):
    return sum(ref[at + k : at + k + 1, :].astype(F32) for k in range(3))


def ends_kernel(proj, cot, to_end, growth, total, ends):
    in_map = proj[:, WIDTH : WIDTH + STATE]
    out_map = proj[:, WIDTH + STATE :]
    fed = [
        (proj[:, head(h)].astype(F32) * to_end[:, h : h + 1]).astype(BF16) for h in range(HEADS)
    ]
    grown = [
        (cot[:, head(h)].astype(F32) * growth[:, h : h + 1]).astype(BF16) for h in range(HEADS)
    ]
    ends[:STATE, :] = mm(in_map, jnp.concatenate(fed, axis=1), TN).astype(BF16)
    ends[STATE : 2 * STATE, :] = mm(out_map, jnp.concatenate(grown, axis=1), TN).astype(BF16)
    ends[2 * STATE :, :] = jnp.zeros((EXTRA, WIDTH), BF16)
    split(total[...], 2 * STATE, ends)


def pair_kernel(place, ends, near, for_x, for_y):
    own_total, near_total = whole(ends, 2 * STATE), whole(near, 2 * STATE)
    is_first = place[0] == 0
    one = jnp.ones_like(own_total)
    decay_own, decay_near = jnp.exp(own_total), jnp.exp(near_total)
    forward = ends[:STATE, :].astype(F32) * jnp.where(is_first, decay_near, one) + near[
        :STATE, :
    ].astype(F32) * jnp.where(is_first, one, decay_own)
    backward = ends[STATE : 2 * STATE, :].astype(F32) * jnp.where(is_first, one, decay_near) + near[
        STATE : 2 * STATE, :
    ].astype(F32) * jnp.where(is_first, decay_own, one)
    for out, low in ((for_x, place[1] % 2 == 0), (for_y, place[1] < 2)):
        out[:STATE, :] = jnp.where(low, forward, backward).astype(BF16)
        out[STATE:, :] = jnp.zeros((EXTRA, WIDTH), BF16)
        split(own_total + near_total, STATE, out)


def local_kernel(
    proj, cot, cum, cum_rows, step_rows, to_end, growth, y, dx, db, dc, fed, grown
):
    rows = proj.shape[0]
    for h in range(HEADS):
        fed[:, head(h)] = (proj[:, head(h)].astype(F32) * to_end[:, h : h + 1]).astype(BF16)
        grown[:, head(h)] = (cot[:, head(h)].astype(F32) * growth[:, h : h + 1]).astype(BF16)
    dx[...] = jnp.zeros_like(dx)
    db[...] = jnp.zeros_like(db)
    for at in range(0, rows, STRIP):
        upto = at + STRIP
        here = slice(at, upto)
        in_map = proj[:upto, WIDTH : WIDTH + STATE]
        out_map = proj[here, WIDTH + STATE :]
        scores = mm(out_map, in_map, NT)
        t = lax.broadcasted_iota(jnp.int32, (STRIP, upto), 0) + at
        s = lax.broadcasted_iota(jnp.int32, (STRIP, upto), 1)
        causal = t >= s
        dscores = jnp.zeros_like(scores)
        for h in range(HEADS):
            span = cum[here, h : h + 1] - cum_rows[h : h + 1, :upto]
            factor = jnp.exp(jnp.where(causal, span, -1e30)) * step_rows[h : h + 1, :upto]
            mixing = (scores * factor).astype(BF16)
            values = proj[:upto, head(h)]
            grad = cot[here, head(h)]
            y[here, head(h)] = mm(mixing, values)
            dx[:upto, head(h)] += mm(mixing, grad, TN)
            dscores = dscores + mm(grad, values, NT) * factor
        dscores = dscores.astype(BF16)
        dc[here, :] = mm(dscores, in_map)
        db[:upto, :] += mm(dscores, out_map, TN)


def enter(place, ends, near, far):
    core, chip = place[0], place[1]
    own_total, near_total = whole(ends, 2 * STATE), whole(near, 2 * STATE)
    sums = [own_total + near_total] + [whole(part, STATE) for part in far]
    of_chip = [
        sum(jnp.where((chip ^ bit) == j, sums[bit], 0.0) for bit in range(4)) for j in range(4)
    ]
    decay = jnp.exp(near_total)
    before = jnp.zeros((STATE, WIDTH), F32)
    after = jnp.zeros((STATE, WIDTH), F32)
    for bit in (1, 2, 3):
        there = chip ^ bit
        low, high = jnp.minimum(chip, there), jnp.maximum(chip, there)
        between = sum(jnp.where((j > low) & (j < high), of_chip[j], 0.0) for j in range(4))
        weight = jnp.exp(between)
        value = far[bit - 1][:STATE, :].astype(F32) * weight
        before = before + jnp.where(there < chip, value, 0.0)
        after = after + jnp.where(there > chip, value, 0.0)
    before = jnp.where(core == 1, before * decay + near[:STATE, :].astype(F32), before)
    after = jnp.where(core == 0, after * decay + near[STATE : 2 * STATE, :].astype(F32), after)
    return before.astype(BF16), after.astype(BF16)


def join_kernel(square, place, proj, to_end, dx, db, dc, fed, grown, *rest):
    ends, (proj_grad, turned, entering) = rest[:-3], rest[-3:]
    if square:
        before, after = enter(place, ends[0], ends[1], ends[2:])
    else:
        before, after = ends[0][:STATE, :], ends[0][STATE:, :]
    entering[...] = before
    carried = mm(proj[:, WIDTH : WIDTH + STATE], after)
    for h in range(HEADS):
        proj_grad[:, head(h)] = (dx[:, head(h)] + carried[:, head(h)] * to_end[:, h : h + 1]).astype(BF16)
    proj_grad[:, WIDTH : WIDTH + STATE] = (db[...] + mm(fed[...], after, NT)).astype(BF16)
    proj_grad[:, WIDTH + STATE :] = (dc[...] + mm(grown[...], before, NT)).astype(BF16)
    turned[...] = proj_grad[...].T


def output_kernel(proj, entering, growth, y, out):
    carried = mm(proj[:, WIDTH + STATE :], entering[...])
    for h in range(HEADS):
        out[:, head(h)] = y[:, head(h)] + carried[:, head(h)] * growth[:, h : h + 1]


def swap(value, size, bit):
    return lax.ppermute(value, "seq", [(i, i ^ bit) for i in range(size)])


def once(value, *others):
    return lax.optimization_barrier((value, *others))[0]


def reduce_on_line(weights, grad, group, beside):
    weights = weights.reshape(4, -1, weights.shape[-1])
    low = group < 2

    def product(at):
        return mm(lax.dynamic_index_in_dim(weights, at, 0, keepdims=False), grad)

    def send(value, pairs):
        return lax.ppermute(value.astype(BF16), "fsdp", pairs)

    inward, across, outward = [(0, 1), (3, 2)], [(1, 2), (2, 1)], [(1, 0), (2, 3)]
    far = product(jnp.where(low, 3, 0)).astype(BF16)
    middle = product(jnp.where(low, 2, 1)).astype(BF16)
    near = product(group ^ 1).astype(BF16)
    far_in, middle_in, near_in = send(far, inward), send(middle, inward), send(near, inward)
    beside[0]((far, middle, near))
    far_in = once(far_in, *beside[1]())
    far_across = send(far.astype(F32) + far_in.astype(F32), across)
    middle_in = once(middle_in, *beside[2]())
    middle_across = send(middle.astype(F32) + middle_in.astype(F32), across)
    far_out = send(near.astype(F32) + far_across.astype(F32), outward)
    own = once(product(group), *beside[3]())
    own, near_in, middle_across, far_out = lax.optimization_barrier((own, near_in, middle_across, far_out))
    return (own + near_in.astype(F32) + middle_across.astype(F32) + far_out.astype(F32)).astype(BF16)


def spread(row):
    return jnp.repeat(row, HEAD_DIM, axis=-1)


def shards(tokens, w_in, step_logit, decay_logit, cotangent):
    size = lax.axis_size("seq")
    me = lax.axis_index("seq")
    core, chip = me % 2, me // 2
    square = size == 8
    rows, columns = tokens.shape[0], w_in.shape[1]
    part = w_in.shape[0]
    half = part // 2
    state = jax.ShapeDtypeStruct

    place = jnp.stack([core, chip]).astype(jnp.int32)

    if square:
        from_x, from_y = swap(w_in, size, 2), swap(w_in, size, 4)
        near = swap(w_in, size, 1)
        corner = jnp.concatenate([swap(from_x[:half], size, 4), swap(from_y[half:], size, 2)])
        near_x, near_y, near_corner = swap(from_x, size, 1), swap(from_y, size, 1), swap(corner, size, 1)
        pieces = [(0, w_in), (1, near), (2, from_x), (4, from_y), (3, near_x), (5, near_y)]
        pieces += [(6, corner), (7, near_corner)]
        ordered = jnp.concatenate(
            [
                lax.dynamic_slice_in_dim(tokens, (me ^ bit) * part, part, axis=1)
                for bit in (1, 3, 5, 7, 0, 2, 4, 6)
            ],
            axis=1,
        )
        to_near, to_keep = ordered[:, : 4 * part], ordered[:, 4 * part :]
        near_tokens = swap(to_near, size, 1)
        total = 0.0
        for bit, piece in pieces:
            at = (bit // 2 + (0 if bit % 2 else 4)) * part
            total = total + mm(ordered[:, at : at + part], piece)
        projected = total.astype(BF16)
        gathered = jnp.zeros((size, part, columns), BF16)
        for bit, piece in pieces:
            gathered = lax.dynamic_update_slice(gathered, piece[None], (me ^ bit, 0, 0))
    else:
        gathered = lax.all_gather(w_in, "seq", axis=0, tiled=True)
        projected = mm(tokens, gathered).astype(BF16)
        gathered = gathered.reshape(size, part, columns)

    step_size = jax.nn.softplus(step_logit)
    log_decay = -jax.nn.softplus(decay_logit)
    lower = (
        lax.broadcasted_iota(jnp.int32, (rows, rows), 0) >= lax.broadcasted_iota(jnp.int32, (rows, rows), 1)
    ).astype(F32)
    cum = lax.dot_general(lower, log_decay, NN, precision=lax.Precision.HIGHEST, preferred_element_type=F32)
    log_total = cum[-1]
    growth = jnp.exp(cum)
    to_end = jnp.exp(log_total[None] - cum) * step_size
    cum_rows, step_rows = cum.T, step_size.T
    (ends,) = call(
        ends_kernel,
        [state((2 * STATE + EXTRA, WIDTH), BF16)],
        [projected, cotangent, to_end, growth, spread(log_total)[None]],
        4 * rows * STATE * WIDTH,
    )
    if square:
        near = swap(ends, size, 1)
        for_x, for_y = call(
            pair_kernel, [state((STATE + EXTRA, WIDTH), BF16)] * 2, [ends, near], 0, place
        )
        ends = [ends, near, swap(for_x, size, 2), swap(for_y, size, 4), swap(for_y, size, 6)]
    else:
        everything = lax.all_gather(ends[: 2 * STATE], "seq")
        totals = lax.all_gather(log_total, "seq")
        places = jnp.arange(size)
        until = jnp.stack([jnp.sum(jnp.where((places < k)[:, None], totals, 0.0), axis=0) for k in range(size + 1)])
        reach = jnp.where((places < me)[:, None], until[me][None] - until[1:], -1e30)
        before = jnp.einsum("jnk,jk->nk", everything[:, :STATE].astype(F32), spread(jnp.exp(reach)))
        reach = jnp.where((places > me)[:, None], until[:-1] - until[me + 1][None], -1e30)
        after = jnp.einsum("jnk,jk->nk", everything[:, STATE:].astype(F32), spread(jnp.exp(reach)))
        ends = [jnp.concatenate([before, after]).astype(BF16)]

    y, dx, db, dc, fed, grown = call(
        local_kernel,
        [
            state((rows, WIDTH), F32),
            state((rows, WIDTH), F32),
            state((rows, STATE), F32),
            state((rows, STATE), F32),
            state((rows, WIDTH), BF16),
            state((rows, WIDTH), BF16),
        ],
        [projected, cotangent, cum, cum_rows, step_rows, to_end, growth],
        20 * rows * rows * STATE,
    )
    dx, gathered = lax.optimization_barrier((dx, gathered))
    proj_grad, turned, entering = call(
        functools.partial(join_kernel, square),
        [state((rows, columns), BF16), state((columns, rows), BF16), state((STATE, WIDTH), BF16)],
        [projected, to_end, dx, db, dc, fed, grown, *ends],
        6 * rows * STATE * WIDTH,
        place,
    )
    groups, group = lax.axis_size("fsdp"), lax.axis_index("fsdp")
    kept, sent, out = [], [], []

    def near_gradient(last):
        kept.append(swap(proj_grad, size, 1))

    def kept_products():
        kept[0] = (mm(to_keep, proj_grad, TN) + mm(near_tokens, kept[0], TN)).astype(BF16)
        own, for_x, for_y, for_corner = kept[0].reshape(4, part, columns)
        sent.extend((own, for_x, for_y, swap(for_corner[:half], size, 2), swap(for_corner[half:], size, 4)))
        sent.extend((swap(for_x[:half], size, 2), swap(for_y[half:], size, 4)))
        return (kept[0],)

    def corner_sums():
        own, for_x, for_y, corner_x, corner_y, top, low = sent
        last_x = (for_x[half:].astype(F32) + corner_y.astype(F32)).astype(BF16)
        last_y = (for_y[:half].astype(F32) + corner_x.astype(F32)).astype(BF16)
        sent.extend((swap(last_x, size, 2), swap(last_y, size, 4)))
        return last_x, last_y

    def outputs():
        out.extend(
            call(
                output_kernel,
                [state((rows, WIDTH), F32)],
                [projected, entering, growth, y],
                2 * rows * STATE * WIDTH,
            )
        )
        return tuple(out)

    if square and groups == 4:
        input_grad = reduce_on_line(gathered, turned, group, (near_gradient, kept_products, corner_sums, outputs))
    else:
        input_grad = lax.psum_scatter(
            mm(gathered.reshape(part * size, columns), turned).astype(BF16), "fsdp", scatter_dimension=0, tiled=True
        )
        outputs()
    (layer_out,) = out

    if square and groups == 4:
        own, for_x, for_y, corner_x, corner_y, top, low, low_x, top_y = sent
        w_in_grad = jnp.concatenate(
            [
                own[:half].astype(F32) + top.astype(F32) + top_y.astype(F32),
                own[half:].astype(F32) + low.astype(F32) + low_x.astype(F32),
            ]
        )
    else:
        w_in_grad = lax.psum_scatter(
            mm(tokens, proj_grad, TN).astype(BF16), "seq", scatter_dimension=0, tiled=True
        ).astype(F32)
    return (layer_out, input_grad, w_in_grad)


def solution(mesh):
    across = P("seq", "fsdp")
    return jax.shard_map(
        shards,
        mesh=mesh,
        in_specs=(P("seq", None), across, across, across, across),
        out_specs=(across, P("fsdp", "seq"), across),
        check_vma=False,
    )
```
